512 devices in a mesh: dom: 64 (over z, y), feat: 8 (over x, core).
Axes of the slice: x: 4, y: 4, z: 16, core: 2. Of those that a mesh axis runs over, the one named last changes fastest.
Arguments:
- features: bfloat16 [65536, 1024], P('dom', 'feat'), may hold values from -6 to 6
- history: bfloat16 [65536, 1024], P('dom', 'feat'), may hold values from -6 to 6
- w_root: bfloat16 [1024, 1024], P(None, 'feat'), may hold values from -0.1875 to 0.1875
- w_neigh: bfloat16 [1024, 1024], P(None, 'feat'), may hold values from -0.1875 to 0.1875
- bias: bfloat16 [1024], P('feat'), may hold values from -3 to 3
- local_tiles: bfloat16 [512, 128, 128], P('dom'), may hold values from -0.25 to 0.25
- halo_tiles: bfloat16 [512, 3, 128, 128], P('dom'), may hold values from -0.25 to 0.25
- local_src: int32 [512], P('dom'), may hold values from 0 to 7
- halo_src: int32 [512, 3], P('dom'), may hold values from 0 to 63
- halo_count: int32 [512], P('dom'), may hold values from 1 to 3
- halo_peer: int32 [4096, 1], P('dom'), may hold values from 0 to 62; in each aligned block of 64 rows (0 to 63, 64 to 127, ...) at most 2 rows name the same one
- halo_block: int32 [4096], P('dom'), may hold values from 0 to 7
Outputs:
- output: bfloat16 [65536, 1024], P('dom', 'feat')
The draws below stay inside these ranges and needn't reach their ends.
Inputs may be any that keep to these rules, and one draw needn't show every extreme that they name: `halo_peer`: among the 64 slots of one partition no offset appears more than 2 times, and some offset appears exactly 2 times; offset r names partition (p + 1 + r) mod 64, never p itself. Halo tiles j >= halo_count[b] of a target block are unused.
All inputs are finite; a program needn't handle non-finite values.
Results may differ from the reference program's by a relative error of at most 0.0037.
Values may be sent and summed in bfloat16 or wider, within the bound.
No kernel may reach another device: no remote copies, remote signals or barrier semaphores. Data moves between devices by JAX's collectives and lax.ppermute only.
A program may use at most 64 MiB of HBM per device.

```python
import math
import jax
import jax.numpy as jnp
import numpy as np
from jax import lax

H = 1024
BLK = 128
TB = 8
HT = 3
HIST_BLK = 8
CAP = 2
HALO = 64
NODES = 65536
TARGET_BLOCKS = 512
HIST_NODES = 65536
HALO_ALL = 4096
N_DOM = 64


def set_ends(drawn, key, smallest, largest):
    longest = drawn.shape.index(max(drawn.shape))
    spots = []
    for shift in (0, 1):
        where = [jax.random.randint(jax.random.fold_in(key, axis), (), 0, length) for axis, length in enumerate(drawn.shape)]
        where[longest] = (where[longest] + shift) % drawn.shape[longest]
        spots.append(tuple(where))
    return drawn.at[spots[0]].set(smallest).at[spots[1]].set(largest)


def block_levels(key, dims, split, smallest, top_value):
    def one(axis_at, shards_of):
        heights = jax.random.uniform(jax.random.fold_in(jax.random.fold_in(key, 6), axis_at), (shards_of,), jnp.float32, smallest / len(split), top_value / len(split))
        return jnp.repeat(jnp.exp(heights), dims[axis_at] // shards_of).reshape((-1,) + (1,) * (len(dims) - axis_at - 1))

    level = one(*split[0])
    for cut in split[1:]:
        level = level * one(*cut)
    return level


def deal_out(own_key, own, number, rows, amount, top, reach, slope):
    ranking = jax.random.permutation(own_key, amount)
    crowded, usual = portions_of(amount, rows * top, reach, slope, True), portions_of(amount, rows * top, reach, slope, False)
    places = jnp.arange(amount)

    def named(sizes, rotation):
        used = int((sizes > 0).sum())
        fixed = max(1, used // 4)
        shifted = fixed + (places - fixed + rotation * (used - fixed)) % max(1, amount - fixed)
        return jnp.zeros((amount,), jnp.int32).at[ranking[jnp.where(places < fixed, places, shifted)]].set(jnp.asarray(sizes, jnp.int32))

    sizes = jnp.where(number % 4 == 0, named(crowded, number // 4), named(usual, number - number // 4 - 1))
    mixed = jax.random.permutation(jax.random.fold_in(own, 3), amount)
    source_of, receiver = mixed[0:amount // 2 * 2:2], mixed[1:amount // 2 * 2:2]
    slack = jnp.minimum(sizes[source_of] - 1, reach - sizes[receiver]) // 2
    slack = jnp.where((source_of == ranking[0]) | (receiver == ranking[0]) | (sizes[receiver] == 0), 0, jnp.maximum(slack, 0))
    shifted = jax.random.randint(jax.random.fold_in(own, 4), (amount // 2,), 0, 1 << 20) % (slack + 1)
    sizes = sizes.at[source_of].add(-shifted).at[receiver].add(shifted)
    items = jnp.searchsorted(jnp.cumsum(sizes), jnp.arange(rows * top), side="right").astype(jnp.int32)
    grid = items.reshape(top, rows).T
    grid = grid[jax.random.permutation(jax.random.fold_in(own, 1), rows)]
    rotation = jax.random.randint(jax.random.fold_in(own, 2), (rows, 1), 0, top)
    return jnp.take_along_axis(grid, (jnp.arange(top)[None, :] + rotation) % top, axis=1)


def portions_of(amount, total, most, skew, full):
    portions = [(1 << 20) // math.isqrt(grade ** skew) + 1 for grade in range(1, amount + 1)]
    largest = most if full else min(most, max(-(-total // amount), total * portions[0] // sum(portions)))
    least = 1 if total - largest >= amount - 1 else 0
    holding, rest = [largest] + [least] * (amount - 1), total - largest - least * (amount - 1)
    while rest > 0:
        movable = [i for i in range(1, amount) if holding[i] < largest] or [i for i in range(1, amount) if holding[i] < most]
        pool, left = sum([portions[i] for i in movable]), rest
        for i in movable:
            extra = min(most - holding[i], max(1, left * portions[i] // pool), rest)
            holding[i] = holding[i] + extra
            rest = rest - extra
    return np.array(holding)


def scatter_about(stream_key, shape, scale, most, split=(), kind=jnp.bfloat16):
    drawn = jax.random.normal(stream_key, shape, jnp.float32) * scale
    if len(split) > 0:
        drawn = block_levels(stream_key, shape, split, -0.22, 0.18) * drawn
    return jnp.clip(drawn, min=-most, max=most).astype(kind)


def setup_inputs(seed: int = 0) -> dict:
    keys = jax.random.split(jax.random.key(seed), 13)
    features = scatter_about(keys[0], (NODES, H), 1.0, 6.0, ((0, 64), (1, 8)))
    history = scatter_about(keys[1], (HIST_NODES, H), 1.0, 6.0, ((0, 64), (1, 8)))
    w_root = scatter_about(keys[2], (H, H), H ** -0.5, 0.1875, ((1, 8),))
    w_neigh = scatter_about(keys[3], (H, H), H ** -0.5, 0.1875, ((1, 8),))
    bias = scatter_about(keys[4], (H,), 0.5, 3.0, ((0, 8),))
    local_tiles = scatter_about(keys[5], (TARGET_BLOCKS, BLK, BLK), (BLK * (1 + HT)) ** -0.5, 0.25, ((0, 64),))
    halo_tiles = scatter_about(keys[6], (TARGET_BLOCKS, HT, BLK, BLK), (BLK * (1 + HT)) ** -0.5, 0.25, ((0, 64),))
    local_src = set_ends(jax.random.randint(keys[7], (TARGET_BLOCKS,), 0, TB), jax.random.fold_in(keys[7], 1), 0, TB - 1).astype(jnp.int32)
    halo_src = set_ends(jax.random.randint(keys[8], (TARGET_BLOCKS, HT), 0, HALO), jax.random.fold_in(keys[8], 1), 0, HALO - 1).astype(jnp.int32)
    halo_count = set_ends(jax.random.randint(keys[9], (TARGET_BLOCKS,), 1, HT + 1), jax.random.fold_in(keys[9], 1), 1, HT).astype(jnp.int32)
    halo_peer_keys = jax.random.split(jax.random.fold_in(keys[10], 1), HALO_ALL // HALO)
    halo_peer_turns = jax.random.permutation(jax.random.fold_in(keys[10], 3), HALO_ALL // HALO)
    halo_peer = jax.vmap(lambda own, number: deal_out(jax.random.fold_in(keys[10], 2), own, number, HALO, N_DOM - 1, 1, CAP, 2))(halo_peer_keys, halo_peer_turns).reshape((HALO_ALL, 1))
    halo_block = set_ends(jax.random.randint(keys[11], (HALO_ALL,), 0, HIST_BLK), jax.random.fold_in(keys[11], 1), 0, HIST_BLK - 1).astype(jnp.int32)
    return {"features": features, "history": history, "w_root": w_root, "w_neigh": w_neigh, "bias": bias, "local_tiles": local_tiles, "halo_tiles": halo_tiles, "local_src": local_src, "halo_src": halo_src, "halo_count": halo_count, "halo_peer": halo_peer, "halo_block": halo_block}


def reference(features, history, w_root, w_neigh, bias, local_tiles, halo_tiles, local_src, halo_src, halo_count, halo_peer, halo_block):
    stored = history.reshape(N_DOM, HIST_BLK, BLK, H)
    root_w = w_root.astype(jnp.float32)
    neigh_w = w_neigh.astype(jnp.float32)
    bias_f = bias.astype(jnp.float32)

    def one_partition(packed):
        partition, own_feats, local_tile, halo_tile, local_index, halo_index, counts, peers, block_ids = packed
        owners = (partition + 1 + peers[:, 0]) % N_DOM
        halo_rows = stored[owners, block_ids].astype(jnp.float32)
        own_blocks = own_feats.reshape(TB, BLK, H).astype(jnp.float32)
        local_part = jnp.einsum("bij,bjc->bic", local_tile.astype(jnp.float32), own_blocks[local_index])
        active = jnp.arange(HT, dtype=jnp.int32)[None, :] < counts[:, None]
        masked = jnp.where(active[:, :, None, None], halo_tile.astype(jnp.float32), jnp.float32(0.0))
        halo_part = jnp.einsum("bkij,bkjc->bic", masked, halo_rows[halo_index])
        aggregate = (local_part + halo_part).astype(jnp.bfloat16).reshape(TB * BLK, H)
        mixed = jnp.dot(own_feats.astype(jnp.float32), root_w) + jnp.dot(aggregate.astype(jnp.float32), neigh_w) + bias_f
        return jax.nn.relu(mixed).astype(jnp.bfloat16)

    packed = (
        jnp.arange(N_DOM, dtype=jnp.int32),
        features.reshape(N_DOM, TB * BLK, H),
        local_tiles.reshape(N_DOM, TB, BLK, BLK),
        halo_tiles.reshape(N_DOM, TB, HT, BLK, BLK),
        local_src.reshape(N_DOM, TB).astype(jnp.int32),
        halo_src.reshape(N_DOM, TB, HT).astype(jnp.int32),
        halo_count.reshape(N_DOM, TB).astype(jnp.int32),
        halo_peer.reshape(N_DOM, HALO, 1).astype(jnp.int32),
        halo_block.reshape(N_DOM, HALO).astype(jnp.int32),
    )
    result = lax.map(one_partition, packed)
    return result.reshape(N_DOM * TB * BLK, H)
```

```python
import jax
import jax.numpy as jnp
from jax import lax
from jax.experimental import pallas as pl
from jax.experimental.pallas import tpu as pltpu
from jax.sharding import Mesh
from jax.sharding import PartitionSpec as P

Z, Y, X, CORE = 16, 4, 4, 2
BLK = 128
TB = 8
HT = 3
REFS = TB * HT
HALF = REFS // CORE
META = 16
GROUP = 4


def pick_kernel(count, slot, core, mine, other, picked, sem):
    def copy(peer, i, tiles):
        row = pl.multiple_of(slot[peer, i] % HALF * BLK, BLK)
        return pltpu.make_async_copy(tiles.at[peer, pl.ds(row, BLK)], picked.at[peer, i], sem.at[peer, i])

    for peer in range(Y):

        @pl.loop(0, count[peer])
        def _(i):
            from_mine = slot[peer, i] // HALF == core[0]

            @pl.when(from_mine)
            def _():
                copy(peer, i, mine).start()

            @pl.when(jnp.logical_not(from_mine))
            def _():
                copy(peer, i, other).start()

    for peer in range(Y):

        @pl.loop(0, count[peer])
        def _(i):
            copy(peer, i, mine).wait()


def partial_kernel(
    count, source, target, me, blocks, tiles, sent, own, block_buf, tile_buf, sent_buf, total, block_sem, tile_sem, out_sem
):
    def groups(peer):
        return (count[peer] + GROUP - 1) // GROUP

    def block_copy(peer, i):
        row = pl.multiple_of(source[peer, i] * BLK, BLK)
        return pltpu.make_async_copy(blocks.at[pl.ds(row, BLK)], block_buf.at[peer, i], block_sem.at[peer, i])

    def tile_copy(peer, group):
        at = pl.ds(group * GROUP, GROUP)
        return pltpu.make_async_copy(tiles.at[peer, at], tile_buf.at[peer, at], tile_sem.at[peer, group])

    for peer in range(Y):

        @pl.loop(0, groups(peer))
        def _(group):
            tile_copy(peer, group).start()
            for u in range(GROUP):
                i = group * GROUP + u

                @pl.when(i < count[peer])
                def _():
                    block_copy(peer, i).start()

    total[...] = jnp.zeros_like(total)
    copies = []
    for peer in range(Y):

        @pl.loop(0, groups(peer))
        def _(group):
            members = [group * GROUP + u for u in range(GROUP)]
            tile_copy(peer, group).wait()
            for i in members:

                @pl.when(i < count[peer])
                def _():
                    block_copy(peer, i).wait()

            products = [
                jnp.dot(tile_buf[peer, i], block_buf[peer, i], preferred_element_type=jnp.float32) for i in members
            ]
            for i, part in zip(members, products):
                total[target[peer, i]] += part

        at = pl.ds(peer * TB, TB)
        sent_buf[at] = jnp.where(me[0] == peer, 0.0, total[at]).astype(sent.dtype)
        copies.append(pltpu.make_async_copy(sent_buf.at[at], sent.at[at], out_sem.at[peer]))
        copies[-1].start()
    copies.append(pltpu.make_async_copy(total.at[pl.ds(me[0] * TB, TB)], own, out_sem.at[Y]))
    copies[-1].start()
    for copy in copies:
        copy.wait()


def partial_sums(place, me, core, blocks, mine, other):
    active = place >= 0
    rank = jnp.cumsum(active.astype(jnp.int32), axis=1) - 1
    numbers = jnp.arange(REFS, dtype=jnp.int32)
    hits = jnp.logical_and(active, rank == numbers[:, None, None])
    count = jnp.sum(active.astype(jnp.int32), axis=1)

    def listed(values, spare):
        return (jnp.sum(jnp.where(hits, values - spare, 0), axis=2) + spare).T

    smem, hbm, vmem = (pl.BlockSpec(memory_space=m) for m in (pltpu.SMEM, pltpu.HBM, pltpu.VMEM))
    picked = pl.pallas_call(
        pick_kernel,
        out_shape=jax.ShapeDtypeStruct((Y, REFS, BLK, BLK), jnp.bfloat16),
        in_specs=[smem] * 3 + [hbm] * 2,
        out_specs=vmem,
        scratch_shapes=[pltpu.SemaphoreType.DMA((Y, REFS))],
        compiler_params=pltpu.CompilerParams(vmem_limit_bytes=8 * 1024 * 1024),
        cost_estimate=pl.CostEstimate(flops=0, bytes_accessed=4 * 2**20, transcendentals=0),
        name="pick_tiles",
    )(count, listed(numbers, 0), core, mine, other)
    return pl.pallas_call(
        partial_kernel,
        out_shape=(
            jax.ShapeDtypeStruct((Y * TB, BLK, BLK), jnp.bfloat16),
            jax.ShapeDtypeStruct((TB, BLK, BLK), jnp.float32),
        ),
        in_specs=[smem] * 4 + [hbm] * 2,
        out_specs=(hbm, hbm),
        scratch_shapes=[
            pltpu.VMEM((Y, REFS, BLK, BLK), jnp.bfloat16),
            pltpu.VMEM((Y, REFS, BLK, BLK), jnp.bfloat16),
            pltpu.VMEM((Y * TB, BLK, BLK), jnp.bfloat16),
            pltpu.VMEM((Y * TB + 1, BLK, BLK), jnp.float32),
            pltpu.SemaphoreType.DMA((Y, REFS)),
            pltpu.SemaphoreType.DMA((Y, REFS // GROUP)),
            pltpu.SemaphoreType.DMA((Y + 1,)),
        ],
        compiler_params=pltpu.CompilerParams(vmem_limit_bytes=60 * 1024 * 1024),
        cost_estimate=pl.CostEstimate(flops=REFS * 2 * BLK**3, bytes_accessed=4 * 2**20, transcendentals=0),
        name="partial_sums",
    )(
        count,
        listed(place, 0),
        listed(numbers // HT + TB * jnp.arange(Y, dtype=jnp.int32)[:, None], Y * TB),
        me,
        blocks,
        picked,
    )


def product_kernel(mine, other, weight, out):
    rows = 256

    @pl.loop(0, out.shape[0] // rows)
    def _(step):
        at = pl.ds(pl.multiple_of(step * rows, rows), rows)
        total = None
        for i in range(X):
            pair = jnp.concatenate([mine[i, at], other[i, at]], axis=1)
            part = jnp.dot(pair, weight[i], preferred_element_type=jnp.float32)
            total = part if total is None else total + part
        out[at] = total.astype(out.dtype)


def product(gathered, weight, dtype):
    mine, other = gathered
    shape = (mine.shape[1], weight.shape[-1])
    vmem = pl.BlockSpec(memory_space=pltpu.VMEM)
    return pl.pallas_call(
        product_kernel,
        out_shape=jax.ShapeDtypeStruct(shape, dtype),
        in_specs=[vmem] * 3,
        out_specs=vmem,
        compiler_params=pltpu.CompilerParams(vmem_limit_bytes=16 * 1024 * 1024),
        cost_estimate=pl.CostEstimate(flops=2 * shape[0] * 1024 * shape[1], bytes_accessed=4 * 2**20, transcendentals=0),
        name="product",
    )(mine, other, weight)


def own_core_first(weight, core):
    parts = weight.reshape(X, CORE, -1, weight.shape[1])
    return jnp.where(core == 0, parts, parts[:, ::-1]).reshape(X, -1, weight.shape[1])


def to_all(array, axis, size):
    return lax.all_to_all(jnp.broadcast_to(array[None], (size,) + array.shape), axis, 0, 0, tiled=True)


def swap_cores(array):
    return lax.ppermute(array, "core", [(0, 1), (1, 0)])


def all_columns(array):
    mine = to_all(array, "x", X)
    return mine, swap_cores(mine)


def body(
    features,
    history,
    w_root,
    w_neigh,
    bias,
    local_tiles,
    halo_tiles,
    local_src,
    halo_src,
    halo_count,
    halo_peer,
    halo_block,
):
    rows, columns = features.shape
    my_z, my_y, my_core = lax.axis_index("z"), lax.axis_index("y"), lax.axis_index("core")

    mixed_history = product(all_columns(history), own_core_first(w_neigh, my_core), jnp.bfloat16)
    column_blocks = lax.all_gather(mixed_history, "z", axis=0, tiled=True)

    _, features, w_neigh, halo_tiles, halo_src, halo_count, halo_peer, halo_block = lax.optimization_barrier(
        (mixed_history, features, w_neigh, halo_tiles, halo_src, halo_count, halo_peer, halo_block)
    )

    owners = (my_z * Y + my_y + 1 + halo_peer[:, 0]) % (Z * Y)
    hits = halo_src.reshape(REFS, 1) == jnp.arange(halo_block.shape[0], dtype=jnp.int32)[None, :]
    used = (lax.broadcasted_iota(jnp.int32, (TB, HT), 1) < halo_count[:, None]).reshape(REFS)
    code = jnp.sum(jnp.where(hits, (owners * TB + halo_block)[None, :], 0), axis=1)
    code = jnp.where(used, code, -TB)
    notes = jnp.stack([code // TB, code % TB])
    notes = jnp.pad(notes, ((0, META - 2), (0, BLK - REFS))).astype(jnp.bfloat16)
    share = lax.dynamic_slice_in_dim(halo_tiles.reshape(REFS * BLK, BLK), my_core * HALF * BLK, HALF * BLK)
    mine = to_all(jnp.concatenate([share, notes]), "y", Y)
    other = swap_cores(mine)
    told = mine[:, HALF * BLK : HALF * BLK + 2, :REFS].astype(jnp.int32)
    owner, block = told[:, 0], told[:, 1]
    here = jnp.logical_and(owner >= 0, owner % Y == my_y)
    place = jnp.where(here, owner // Y * TB + block, -1)

    all_features = all_columns(features)
    own_mixed = product(all_features, own_core_first(w_neigh, my_core), jnp.bfloat16).reshape(TB, BLK, columns)
    local_part = jnp.einsum("bij,bjc->bic", local_tiles, own_mixed[local_src], preferred_element_type=jnp.float32)
    root = product(all_features, own_core_first(w_root, my_core), jnp.float32)
    base = root + local_part.reshape(rows, columns) + bias.astype(jnp.float32)

    sent, own = partial_sums(place, my_y.reshape(1), my_core.reshape(1), column_blocks, mine, other)
    came = lax.all_to_all(sent.reshape(Y, rows, columns), "y", 0, 0, tiled=True)
    total = lax.optimization_barrier(base + own.reshape(rows, columns))
    for i in range(Y):
        total = total + came[i].astype(jnp.float32)
    return jax.nn.relu(total).astype(jnp.bfloat16)


def solution(mesh):
    chips = Mesh(mesh.devices.reshape(Z, Y, X, CORE), ("z", "y", "x", "core"))
    dom, feat = ("z", "y"), ("x", "core")
    in_specs = (
        P(dom, feat),
        P(dom, feat),
        P(None, feat),
        P(None, feat),
        P(feat),
        P(dom, None, None),
        P(dom, None, None, None),
        P(dom),
        P(dom, None),
        P(dom),
        P(dom, None),
        P(dom),
    )
    return jax.shard_map(body, mesh=chips, in_specs=in_specs, out_specs=P(dom, feat), check_vma=False)
```

```python
import functools

import jax
import jax.numpy as jnp
from jax import lax
from jax.experimental import pallas as pl
from jax.experimental.pallas import tpu as pltpu
from jax.sharding import Mesh
from jax.sharding import PartitionSpec as P

Z, Y, X, CORE = 16, 4, 4, 2
BLK = 128
TB = 8
HT = 3
REFS = TB * HT
HALF = REFS // CORE
META = 16
GROUP = 4


def pick_kernel(notes, place, mine, other, table, picked, buf, sem, out_sem):
    me, core = place[0], place[1]
    counts = []
    for peer in range(Y):

        def step(ref, count):
            owner, block = notes[peer, ref], notes[peer, REFS + ref]
            here = jnp.logical_and(owner >= 0, lax.rem(owner, Y) == me)
            at = pl.ds(pl.multiple_of(lax.rem(ref, HALF) * BLK, BLK), BLK)
            from_mine = lax.div(ref, HALF) == core

            @pl.when(here)
            def _():
                table[peer, count] = lax.div(owner, Y) * TB + block
                table[peer, REFS + count] = peer * TB + lax.div(ref, HT)

            @pl.when(jnp.logical_and(here, from_mine))
            def _():
                pltpu.make_async_copy(mine.at[peer, at], buf.at[peer, count], sem.at[peer, count]).start()

            @pl.when(jnp.logical_and(here, jnp.logical_not(from_mine)))
            def _():
                pltpu.make_async_copy(other.at[peer, at], buf.at[peer, count], sem.at[peer, count]).start()

            return count + here.astype(jnp.int32)

        count = lax.fori_loop(0, REFS, step, jnp.int32(0))
        counts.append(count)
        table[peer, 2 * REFS] = count
        table[peer, 2 * REFS + 1] = me

        @pl.loop(count, REFS)
        def _(i):
            table[peer, i] = 0
            table[peer, REFS + i] = Y * TB

    def out_copy(peer, group):
        at = pl.ds(group * GROUP, GROUP)
        return pltpu.make_async_copy(buf.at[peer, at], picked.at[peer, at], out_sem.at[peer, group])

    for peer in range(Y):

        @pl.loop(0, (counts[peer] + GROUP - 1) // GROUP)
        def _(group):
            for u in range(GROUP):
                i = group * GROUP + u

                @pl.when(i < counts[peer])
                def _():
                    pltpu.make_async_copy(mine.at[peer, pl.ds(0, BLK)], buf.at[peer, i], sem.at[peer, i]).wait()

            out_copy(peer, group).start()

    for peer in range(Y):

        @pl.loop(0, (counts[peer] + GROUP - 1) // GROUP)
        def _(group):
            out_copy(peer, group).wait()


def partial_kernel(
    table, blocks, tiles, sent, own, block_buf, tile_buf, sent_buf, total, block_sem, tile_sem, out_sem
):
    count = [table[peer, 2 * REFS] for peer in range(Y)]
    me = table[0, 2 * REFS + 1]

    def groups(peer):
        return (count[peer] + GROUP - 1) // GROUP

    def block_copy(peer, i):
        row = pl.multiple_of(table[peer, i] * BLK, BLK)
        return pltpu.make_async_copy(blocks.at[pl.ds(row, BLK)], block_buf.at[peer, i], block_sem.at[peer, i])

    def tile_copy(peer, group):
        at = pl.ds(group * GROUP, GROUP)
        return pltpu.make_async_copy(tiles.at[peer, at], tile_buf.at[peer, at], tile_sem.at[peer, group])

    for peer in range(Y):

        @pl.loop(0, groups(peer))
        def _(group):
            tile_copy(peer, group).start()
            for u in range(GROUP):
                i = group * GROUP + u

                @pl.when(i < count[peer])
                def _():
                    block_copy(peer, i).start()

    total[...] = jnp.zeros_like(total)
    copies = []
    for peer in range(Y):

        @pl.loop(0, groups(peer))
        def _(group):
            members = [group * GROUP + u for u in range(GROUP)]
            tile_copy(peer, group).wait()
            for i in members:

                @pl.when(i < count[peer])
                def _():
                    block_copy(peer, i).wait()

            products = [
                jnp.dot(tile_buf[peer, i], block_buf[peer, i], preferred_element_type=jnp.float32) for i in members
            ]
            for i, part in zip(members, products):
                total[table[peer, REFS + i]] += part

        at = pl.ds(peer * TB, TB)
        sent_buf[at] = jnp.where(me == peer, 0.0, total[at]).astype(sent.dtype)
        copies.append(pltpu.make_async_copy(sent_buf.at[at], sent.at[at], out_sem.at[peer]))
        copies[-1].start()
    copies.append(pltpu.make_async_copy(total.at[pl.ds(me * TB, TB)], own, out_sem.at[Y]))
    copies[-1].start()
    for copy in copies:
        copy.wait()


def partial_sums(notes, place, blocks, mine, other):
    smem, hbm = pl.BlockSpec(memory_space=pltpu.SMEM), pl.BlockSpec(memory_space=pltpu.HBM)
    table, picked = pl.pallas_call(
        pick_kernel,
        out_shape=(
            jax.ShapeDtypeStruct((Y, 2 * REFS + 2), jnp.int32),
            jax.ShapeDtypeStruct((Y, REFS, BLK, BLK), jnp.bfloat16),
        ),
        in_specs=[smem] * 2 + [hbm] * 2,
        out_specs=(smem, hbm),
        scratch_shapes=[
            pltpu.VMEM((Y, REFS, BLK, BLK), jnp.bfloat16),
            pltpu.SemaphoreType.DMA((Y, REFS)),
            pltpu.SemaphoreType.DMA((Y, REFS // GROUP)),
        ],
        compiler_params=pltpu.CompilerParams(vmem_limit_bytes=8 * 1024 * 1024),
        cost_estimate=pl.CostEstimate(flops=0, bytes_accessed=4 * 2**20, transcendentals=0),
        name="pick_tiles",
    )(notes, place, mine, other)
    return pl.pallas_call(
        partial_kernel,
        out_shape=(
            jax.ShapeDtypeStruct((Y * TB, BLK, BLK), jnp.bfloat16),
            jax.ShapeDtypeStruct((TB, BLK, BLK), jnp.float32),
        ),
        in_specs=[smem] + [hbm] * 2,
        out_specs=(hbm, hbm),
        scratch_shapes=[
            pltpu.VMEM((Y, REFS, BLK, BLK), jnp.bfloat16),
            pltpu.VMEM((Y, REFS, BLK, BLK), jnp.bfloat16),
            pltpu.VMEM((Y * TB, BLK, BLK), jnp.bfloat16),
            pltpu.VMEM((Y * TB + 1, BLK, BLK), jnp.float32),
            pltpu.SemaphoreType.DMA((Y, REFS)),
            pltpu.SemaphoreType.DMA((Y, REFS // GROUP)),
            pltpu.SemaphoreType.DMA((Y + 1,)),
        ],
        compiler_params=pltpu.CompilerParams(vmem_limit_bytes=60 * 1024 * 1024),
        cost_estimate=pl.CostEstimate(flops=REFS * 2 * BLK**3, bytes_accessed=4 * 2**20, transcendentals=0),
        name="partial_sums",
    )(table, blocks, picked)


def product_kernel(last, parts, weight, base, out):
    rows = 256

    @pl.loop(0, out.shape[0] // rows)
    def _(step):
        at = pl.ds(pl.multiple_of(step * rows, rows), rows)
        total = base[at]
        for i in range(X // 2):
            pair = jnp.concatenate([parts[2 * i, at], parts[2 * i + 1, at]], axis=1)
            total = total + jnp.dot(pair, weight[i], preferred_element_type=jnp.float32)
        out[at] = jnp.maximum(total, 0.0).astype(out.dtype) if last else total


def add_product(base, parts, weight, last=False):
    vmem = pl.BlockSpec(memory_space=pltpu.VMEM)
    return pl.pallas_call(
        functools.partial(product_kernel, last),
        out_shape=jax.ShapeDtypeStruct(base.shape, jnp.bfloat16 if last else jnp.float32),
        in_specs=[vmem] * 3,
        out_specs=vmem,
        compiler_params=pltpu.CompilerParams(vmem_limit_bytes=16 * 1024 * 1024),
        cost_estimate=pl.CostEstimate(flops=base.size * 1024, bytes_accessed=2 * 2**20, transcendentals=0),
        name="add_product",
    )(parts, weight, base)


def rows_of_core(weight, core):
    parts = weight.reshape(X, CORE, BLK, weight.shape[1])
    return jnp.where(core == 0, parts[:, 0], parts[:, 1]).reshape(X // 2, 2 * BLK, weight.shape[1])


def to_all(array, axis, size):
    return lax.all_to_all(jnp.broadcast_to(array[None], (size,) + array.shape), axis, 0, 0, tiled=True)


def swap_cores(array):
    return lax.ppermute(array, "core", [(0, 1), (1, 0)])


def all_columns(array):
    mine = to_all(array, "x", X)
    return mine, swap_cores(mine)


def body(
    features,
    history,
    w_root,
    w_neigh,
    bias,
    local_tiles,
    halo_tiles,
    local_src,
    halo_src,
    halo_count,
    halo_peer,
    halo_block,
):
    rows, columns = features.shape
    my_z, my_y, my_core = lax.axis_index("z"), lax.axis_index("y"), lax.axis_index("core")

    column_blocks = lax.all_gather(history, "z", axis=0, tiled=True)

    owners = (my_z * Y + my_y + 1 + halo_peer[:, 0]) % (Z * Y)
    hits = halo_src.reshape(REFS, 1) == jnp.arange(halo_block.shape[0], dtype=jnp.int32)[None, :]
    used = (lax.broadcasted_iota(jnp.int32, (TB, HT), 1) < halo_count[:, None]).reshape(REFS)
    code = jnp.sum(jnp.where(hits, (owners * TB + halo_block)[None, :], 0), axis=1)
    code = jnp.where(used, code, -TB)
    notes = jnp.stack([code // TB, code % TB])
    notes = jnp.pad(notes, ((0, META - 2), (0, BLK - REFS))).astype(jnp.bfloat16)
    share = lax.dynamic_slice_in_dim(halo_tiles.reshape(REFS * BLK, BLK), my_core * HALF * BLK, HALF * BLK)
    mine = to_all(jnp.concatenate([share, notes]), "y", Y)
    other = swap_cores(mine)
    told = mine[:, HALF * BLK : HALF * BLK + 2, :REFS].astype(jnp.int32).reshape(Y, 2 * REFS)
    place = jnp.stack([my_y, my_core])

    own_blocks = features.reshape(TB, BLK, columns)[local_src]
    local_part = jnp.einsum("bij,bjc->bic", local_tiles, own_blocks, preferred_element_type=jnp.float32)
    base = jnp.broadcast_to(bias.astype(jnp.float32)[None], (rows, columns))
    mine_f, other_f = all_columns(features)
    base = add_product(base, mine_f, rows_of_core(w_root, my_core))
    base = add_product(base, other_f, rows_of_core(w_root, 1 - my_core))
    neigh, neigh_other = rows_of_core(w_neigh, my_core), rows_of_core(w_neigh, 1 - my_core)
    column_blocks, base, local_part, neigh, neigh_other = lax.optimization_barrier(
        (column_blocks, base, local_part, neigh, neigh_other)
    )

    sent, own = partial_sums(told, place, column_blocks, mine, other)
    came = lax.all_to_all(sent.reshape(Y, rows, columns), "y", 0, 0, tiled=True)
    total = lax.optimization_barrier(local_part + own).reshape(rows, columns)
    for i in range(Y):
        total = total + came[i].astype(jnp.float32)
    mine_a = to_all(total.astype(jnp.bfloat16), "x", X)
    other_a = swap_cores(mine_a)
    base = add_product(base, mine_a, neigh)
    return add_product(base, other_a, neigh_other, last=True)


def solution(mesh):
    chips = Mesh(mesh.devices.reshape(Z, Y, X, CORE), ("z", "y", "x", "core"))
    dom, feat = ("z", "y"), ("x", "core")
    in_specs = (
        P(dom, feat),
        P(dom, feat),
        P(None, feat),
        P(None, feat),
        P(feat),
        P(dom, None, None),
        P(dom, None, None, None),
        P(dom),
        P(dom, None),
        P(dom),
        P(dom, None),
        P(dom),
    )
    return jax.shard_map(body, mesh=chips, in_specs=in_specs, out_specs=P(dom, feat), check_vma=False)
```

```python
import functools

import jax
import jax.numpy as jnp
from jax import lax
from jax.experimental import pallas as pl
from jax.experimental.pallas import tpu as pltpu
from jax.sharding import Mesh
from jax.sharding import PartitionSpec as P

Z, Y, X, CORE = 16, 4, 4, 2
BLK = 128
TB = 8
HT = 3
REFS = TB * HT
HALF = REFS // CORE
META = 16
GROUP = 4


def pick_kernel(notes, place, mine, other, table, picked, buf, sem, out_sem):
    me, core = place[0], place[1]
    counts = []
    for peer in range(Y):

        def step(ref, count):
            owner, block = notes[peer, ref], notes[peer, REFS + ref]
            here = jnp.logical_and(owner >= 0, lax.rem(owner, Y) == me)
            at = pl.ds(pl.multiple_of(lax.rem(ref, HALF) * BLK, BLK), BLK)
            from_mine = lax.div(ref, HALF) == core

            @pl.when(here)
            def _():
                table[peer, count] = lax.div(owner, Y) * TB + block
                table[peer, REFS + count] = peer * TB + lax.div(ref, HT)

            @pl.when(jnp.logical_and(here, from_mine))
            def _():
                pltpu.make_async_copy(mine.at[peer, at], buf.at[peer, count], sem.at[peer, count]).start()

            @pl.when(jnp.logical_and(here, jnp.logical_not(from_mine)))
            def _():
                pltpu.make_async_copy(other.at[peer, at], buf.at[peer, count], sem.at[peer, count]).start()

            return count + here.astype(jnp.int32)

        count = lax.fori_loop(0, REFS, step, jnp.int32(0))
        counts.append(count)
        table[peer, 2 * REFS] = count
        table[peer, 2 * REFS + 1] = me

        @pl.loop(count, REFS)
        def _(i):
            table[peer, i] = 0
            table[peer, REFS + i] = Y * TB

    def out_copy(peer, group):
        at = pl.ds(group * GROUP, GROUP)
        return pltpu.make_async_copy(buf.at[peer, at], picked.at[peer, at], out_sem.at[peer, group])

    for peer in range(Y):

        @pl.loop(0, (counts[peer] + GROUP - 1) // GROUP)
        def _(group):
            for u in range(GROUP):
                i = group * GROUP + u

                @pl.when(i < counts[peer])
                def _():
                    pltpu.make_async_copy(mine.at[peer, pl.ds(0, BLK)], buf.at[peer, i], sem.at[peer, i]).wait()

            out_copy(peer, group).start()

    for peer in range(Y):

        @pl.loop(0, (counts[peer] + GROUP - 1) // GROUP)
        def _(group):
            out_copy(peer, group).wait()


def partial_kernel(
    table, blocks, tiles, local, sent, block_buf, tile_buf, local_buf, sent_buf, total, block_sem, tile_sem, out_sem
):
    count = [table[peer, 2 * REFS] for peer in range(Y)]
    me = table[0, 2 * REFS + 1]

    def groups(peer):
        return (count[peer] + GROUP - 1) // GROUP

    def block_copy(peer, i):
        row = pl.multiple_of(table[peer, i] * BLK, BLK)
        return pltpu.make_async_copy(blocks.at[pl.ds(row, BLK)], block_buf.at[peer, i], block_sem.at[peer, i])

    def tile_copy(peer, group):
        at = pl.ds(group * GROUP, GROUP)
        return pltpu.make_async_copy(tiles.at[peer, at], tile_buf.at[peer, at], tile_sem.at[peer, group])

    for peer in range(Y):

        @pl.loop(0, groups(peer))
        def _(group):
            tile_copy(peer, group).start()
            for u in range(GROUP):
                i = group * GROUP + u

                @pl.when(i < count[peer])
                def _():
                    block_copy(peer, i).start()

    local_copy = pltpu.make_async_copy(local, local_buf, out_sem.at[Y])
    local_copy.start()
    total[...] = jnp.zeros_like(total)
    copies = []
    for peer in range(Y):

        @pl.loop(0, groups(peer))
        def _(group):
            members = [group * GROUP + u for u in range(GROUP)]
            tile_copy(peer, group).wait()
            for i in members:

                @pl.when(i < count[peer])
                def _():
                    block_copy(peer, i).wait()

            products = [
                jnp.dot(tile_buf[peer, i], block_buf[peer, i], preferred_element_type=jnp.float32) for i in members
            ]
            for i, part in zip(members, products):
                total[table[peer, REFS + i]] += part

        @pl.when(me == peer)
        def _():
            local_copy.wait()
            total[pl.ds(peer * TB, TB)] += local_buf[...]

        at = pl.ds(peer * TB, TB)
        sent_buf[at] = total[at].astype(sent.dtype)
        copies.append(pltpu.make_async_copy(sent_buf.at[at], sent.at[at], out_sem.at[peer]))
        copies[-1].start()
    for copy in copies:
        copy.wait()


def partial_sums(notes, place, blocks, local, mine, other):
    smem, hbm = pl.BlockSpec(memory_space=pltpu.SMEM), pl.BlockSpec(memory_space=pltpu.HBM)
    table, picked = pl.pallas_call(
        pick_kernel,
        out_shape=(
            jax.ShapeDtypeStruct((Y, 2 * REFS + 2), jnp.int32),
            jax.ShapeDtypeStruct((Y, REFS, BLK, BLK), jnp.bfloat16),
        ),
        in_specs=[smem] * 2 + [hbm] * 2,
        out_specs=(smem, hbm),
        scratch_shapes=[
            pltpu.VMEM((Y, REFS, BLK, BLK), jnp.bfloat16),
            pltpu.SemaphoreType.DMA((Y, REFS)),
            pltpu.SemaphoreType.DMA((Y, REFS // GROUP)),
        ],
        compiler_params=pltpu.CompilerParams(vmem_limit_bytes=8 * 1024 * 1024),
        cost_estimate=pl.CostEstimate(flops=0, bytes_accessed=4 * 2**20, transcendentals=0),
        name="pick_tiles",
    )(notes, place, mine, other)
    return pl.pallas_call(
        partial_kernel,
        out_shape=jax.ShapeDtypeStruct((Y * TB, BLK, BLK), jnp.bfloat16),
        in_specs=[smem] + [hbm] * 3,
        out_specs=hbm,
        scratch_shapes=[
            pltpu.VMEM((Y, REFS, BLK, BLK), jnp.bfloat16),
            pltpu.VMEM((Y, REFS, BLK, BLK), jnp.bfloat16),
            pltpu.VMEM((TB, BLK, BLK), jnp.float32),
            pltpu.VMEM((Y * TB, BLK, BLK), jnp.bfloat16),
            pltpu.VMEM((Y * TB + 1, BLK, BLK), jnp.float32),
            pltpu.SemaphoreType.DMA((Y, REFS)),
            pltpu.SemaphoreType.DMA((Y, REFS // GROUP)),
            pltpu.SemaphoreType.DMA((Y + 1,)),
        ],
        compiler_params=pltpu.CompilerParams(vmem_limit_bytes=60 * 1024 * 1024),
        cost_estimate=pl.CostEstimate(flops=REFS * 2 * BLK**3, bytes_accessed=4 * 2**20, transcendentals=0),
        name="partial_sums",
    )(table, blocks, picked, local)


def product_kernel(last, parts, weight, base, out):
    pairs = [jnp.concatenate([parts[2 * i], parts[2 * i + 1]], axis=1) for i in range(X // 2)]
    for x in range(X):
        total = base[x]
        for i, pair in enumerate(pairs):
            total = total + jnp.dot(pair, weight[x, i], preferred_element_type=jnp.float32)
        out[x] = jnp.maximum(total, 0.0).astype(out.dtype) if last else total


def add_product(base, parts, weight, last=False):
    vmem = pl.BlockSpec(memory_space=pltpu.VMEM)
    return pl.pallas_call(
        functools.partial(product_kernel, last),
        out_shape=jax.ShapeDtypeStruct(base.shape, jnp.bfloat16 if last else jnp.float32),
        in_specs=[vmem] * 3,
        out_specs=vmem,
        compiler_params=pltpu.CompilerParams(vmem_limit_bytes=16 * 1024 * 1024),
        cost_estimate=pl.CostEstimate(flops=base.size * 1024, bytes_accessed=2 * 2**20, transcendentals=0),
        name="add_product",
    )(parts, weight, base)


def rows_of_core(weights, core):
    parts = weights.reshape(X, X, CORE, BLK, BLK)
    return jnp.where(core == 0, parts[:, :, 0], parts[:, :, 1]).reshape(X, X // 2, 2 * BLK, BLK)


def to_all(array, axis, size):
    return lax.all_to_all(jnp.broadcast_to(array[None], (size,) + array.shape), axis, 0, 0, tiled=True)


def swap_cores(array):
    return lax.ppermute(array, "core", [(0, 1), (1, 0)])


def of_ring(array, x):
    came = [array] + [lax.ppermute(array, "x", [(i, (i + r) % X) for i in range(X)]) for r in range(1, X)]
    return jnp.stack(came)[(x - jnp.arange(X)) % X]


def body(
    features,
    history,
    w_root,
    w_neigh,
    bias,
    local_tiles,
    halo_tiles,
    local_src,
    halo_src,
    halo_count,
    halo_peer,
    halo_block,
):
    rows, columns = features.shape
    my_z, my_y, my_core = lax.axis_index("z"), lax.axis_index("y"), lax.axis_index("core")

    column_blocks = lax.all_gather(history, "z", axis=0, tiled=True)

    depth = w_root.shape[0]
    bias_rows = jnp.pad(bias[None], ((0, META - 1), (0, 0)))
    weights = of_ring(jnp.concatenate([w_root, w_neigh, bias_rows]), lax.axis_index("x"))
    root, neigh, bias_row = weights[:, :depth], weights[:, depth : 2 * depth], weights[:, 2 * depth : 2 * depth + 1]

    owners = (my_z * Y + my_y + 1 + halo_peer[:, 0]) % (Z * Y)
    hits = halo_src.reshape(REFS, 1) == jnp.arange(halo_block.shape[0], dtype=jnp.int32)[None, :]
    used = (lax.broadcasted_iota(jnp.int32, (TB, HT), 1) < halo_count[:, None]).reshape(REFS)
    code = jnp.sum(jnp.where(hits, (owners * TB + halo_block)[None, :], 0), axis=1)
    code = jnp.where(used, code, -TB)
    notes = jnp.stack([code // TB, code % TB])
    notes = jnp.pad(notes, ((0, META - 2), (0, BLK - REFS))).astype(jnp.bfloat16)
    share = lax.dynamic_slice_in_dim(halo_tiles.reshape(REFS * BLK, BLK), my_core * HALF * BLK, HALF * BLK)
    mine = to_all(jnp.concatenate([share, notes]), "y", Y)
    other = swap_cores(mine)
    told = mine[:, HALF * BLK : HALF * BLK + 2, :REFS].astype(jnp.int32).reshape(Y, 2 * REFS)
    place = jnp.stack([my_y, my_core])

    own_blocks = features.reshape(TB, BLK, columns)[local_src]
    local_part = jnp.einsum("bij,bjc->bic", local_tiles, own_blocks, preferred_element_type=jnp.float32)
    quarter = (X, rows // X, columns)
    mine_f = lax.all_to_all(features.reshape(quarter), "x", 0, 0, tiled=True)
    other_f = swap_cores(mine_f)
    base = jnp.broadcast_to(bias_row.astype(jnp.float32), quarter)
    base = add_product(base, mine_f, rows_of_core(root, my_core))
    base = add_product(base, other_f, rows_of_core(root, 1 - my_core))
    neigh_mine, neigh_other = rows_of_core(neigh, my_core), rows_of_core(neigh, 1 - my_core)
    column_blocks, base, local_part, neigh_mine, neigh_other = lax.optimization_barrier(
        (column_blocks, base, local_part, neigh_mine, neigh_other)
    )

    sent = partial_sums(told, place, column_blocks, local_part, mine, other)
    came = lax.all_to_all(sent.reshape((Y * X,) + quarter[1:]), ("y", "x"), 0, 0, tiled=True).astype(jnp.float32)
    aggregate = sum(came[y * X : (y + 1) * X] for y in range(Y)).astype(jnp.bfloat16)
    other_a = swap_cores(aggregate)
    base = add_product(base, aggregate, neigh_mine)
    out = add_product(base, other_a, neigh_other, last=True)
    return lax.all_to_all(out, "x", 0, 0, tiled=True).reshape(rows, columns)


def solution(mesh):
    chips = Mesh(mesh.devices.reshape(Z, Y, X, CORE), ("z", "y", "x", "core"))
    dom, feat = ("z", "y"), ("x", "core")
    in_specs = (
        P(dom, feat),
        P(dom, feat),
        P(None, feat),
        P(None, feat),
        P(feat),
        P(dom, None, None),
        P(dom, None, None, None),
        P(dom),
        P(dom, None),
        P(dom),
        P(dom, None),
        P(dom),
    )
    return jax.shard_map(body, mesh=chips, in_specs=in_specs, out_specs=P(dom, feat), check_vma=False)
```

```python
import functools

import jax
import jax.numpy as jnp
from jax import lax
from jax.experimental import pallas as pl
from jax.experimental.pallas import tpu as pltpu
from jax.sharding import Mesh
from jax.sharding import PartitionSpec as P

Z, Y, X, CORE = 16, 4, 4, 2
BLK = 128
TB = 8
HT = 3
REFS = TB * HT
HALF = REFS // CORE
META = 16
GROUP = 4


def pick_kernel(notes, place, mine, other, table, picked, buf, sem, out_sem):
    me, core = place[0], place[1]
    counts = []
    for peer in range(Y):

        def step(ref, count):
            owner, block = notes[peer, ref], notes[peer, REFS + ref]
            here = jnp.logical_and(owner >= 0, lax.rem(owner, Y) == me)
            at = pl.ds(pl.multiple_of(lax.rem(ref, HALF) * BLK, BLK), BLK)
            from_mine = lax.div(ref, HALF) == core

            @pl.when(here)
            def _():
                table[peer, count] = lax.div(owner, Y) * TB + block
                table[peer, REFS + count] = peer * TB + lax.div(ref, HT)

            @pl.when(jnp.logical_and(here, from_mine))
            def _():
                pltpu.make_async_copy(mine.at[peer, at], buf.at[peer, count], sem.at[peer, count]).start()

            @pl.when(jnp.logical_and(here, jnp.logical_not(from_mine)))
            def _():
                pltpu.make_async_copy(other.at[peer, at], buf.at[peer, count], sem.at[peer, count]).start()

            return count + here.astype(jnp.int32)

        count = lax.fori_loop(0, REFS, step, jnp.int32(0))
        counts.append(count)
        table[peer, 2 * REFS] = count
        table[peer, 2 * REFS + 1] = me

        @pl.loop(count, REFS)
        def _(i):
            table[peer, i] = 0
            table[peer, REFS + i] = Y * TB

    def out_copy(peer, group):
        at = pl.ds(group * GROUP, GROUP)
        return pltpu.make_async_copy(buf.at[peer, at], picked.at[peer, at], out_sem.at[peer, group])

    for peer in range(Y):

        @pl.loop(0, (counts[peer] + GROUP - 1) // GROUP)
        def _(group):
            for u in range(GROUP):
                i = group * GROUP + u

                @pl.when(i < counts[peer])
                def _():
                    pltpu.make_async_copy(mine.at[peer, pl.ds(0, BLK)], buf.at[peer, i], sem.at[peer, i]).wait()

            out_copy(peer, group).start()

    for peer in range(Y):

        @pl.loop(0, (counts[peer] + GROUP - 1) // GROUP)
        def _(group):
            out_copy(peer, group).wait()


def partial_kernel(
    table, blocks, tiles, local, sent, block_buf, tile_buf, local_buf, total, block_sem, tile_sem, local_sem
):
    count = [table[peer, 2 * REFS] for peer in range(Y)]
    me = table[0, 2 * REFS + 1]

    def groups(peer):
        return (count[peer] + GROUP - 1) // GROUP

    def block_copy(peer, i):
        row = pl.multiple_of(table[peer, i] * BLK, BLK)
        return pltpu.make_async_copy(blocks.at[pl.ds(row, BLK)], block_buf.at[peer, i], block_sem.at[peer, i])

    def tile_copy(peer, group):
        at = pl.ds(group * GROUP, GROUP)
        return pltpu.make_async_copy(tiles.at[peer, at], tile_buf.at[peer, at], tile_sem.at[peer, group])

    for peer in range(Y):

        @pl.loop(0, groups(peer))
        def _(group):
            tile_copy(peer, group).start()
            for u in range(GROUP):
                i = group * GROUP + u

                @pl.when(i < count[peer])
                def _():
                    block_copy(peer, i).start()

    local_copy = pltpu.make_async_copy(local, local_buf, local_sem)
    local_copy.start()
    total[...] = jnp.zeros_like(total)
    for peer in range(Y):

        @pl.loop(0, groups(peer))
        def _(group):
            members = [group * GROUP + u for u in range(GROUP)]
            tile_copy(peer, group).wait()
            for i in members:

                @pl.when(i < count[peer])
                def _():
                    block_copy(peer, i).wait()

            products = [
                jnp.dot(tile_buf[peer, i], block_buf[peer, i], preferred_element_type=jnp.float32) for i in members
            ]
            for i, part in zip(members, products):
                total[table[peer, REFS + i]] += part

        @pl.when(me == peer)
        def _():
            local_copy.wait()
            total[pl.ds(peer * TB, TB)] += local_buf[...]

        at = pl.ds(peer * TB, TB)
        sent[at] = total[at].astype(sent.dtype)


def partial_sums(notes, place, blocks, local, mine, other):
    smem, hbm = pl.BlockSpec(memory_space=pltpu.SMEM), pl.BlockSpec(memory_space=pltpu.HBM)
    table, picked = pl.pallas_call(
        pick_kernel,
        out_shape=(
            jax.ShapeDtypeStruct((Y, 2 * REFS + 2), jnp.int32),
            jax.ShapeDtypeStruct((Y, REFS, BLK, BLK), jnp.bfloat16),
        ),
        in_specs=[smem] * 2 + [hbm] * 2,
        out_specs=(smem, hbm),
        scratch_shapes=[
            pltpu.VMEM((Y, REFS, BLK, BLK), jnp.bfloat16),
            pltpu.SemaphoreType.DMA((Y, REFS)),
            pltpu.SemaphoreType.DMA((Y, REFS // GROUP)),
        ],
        compiler_params=pltpu.CompilerParams(vmem_limit_bytes=8 * 1024 * 1024),
        cost_estimate=pl.CostEstimate(flops=0, bytes_accessed=4 * 2**20, transcendentals=0),
        name="pick_tiles",
    )(notes, place, mine, other)
    return pl.pallas_call(
        partial_kernel,
        out_shape=jax.ShapeDtypeStruct((Y * TB, BLK, BLK), jnp.bfloat16),
        in_specs=[smem] + [hbm] * 3,
        out_specs=pl.BlockSpec(memory_space=pltpu.VMEM),
        scratch_shapes=[
            pltpu.VMEM((Y, REFS, BLK, BLK), jnp.bfloat16),
            pltpu.VMEM((Y, REFS, BLK, BLK), jnp.bfloat16),
            pltpu.VMEM((TB, BLK, BLK), jnp.float32),
            pltpu.VMEM((Y * TB + 1, BLK, BLK), jnp.float32),
            pltpu.SemaphoreType.DMA((Y, REFS)),
            pltpu.SemaphoreType.DMA((Y, REFS // GROUP)),
            pltpu.SemaphoreType.DMA,
        ],
        compiler_params=pltpu.CompilerParams(vmem_limit_bytes=60 * 1024 * 1024),
        cost_estimate=pl.CostEstimate(flops=REFS * 2 * BLK**3, bytes_accessed=4 * 2**20, transcendentals=0),
        name="partial_sums",
    )(table, blocks, picked, local)


def product_kernel(last, parts, weight, base, out):
    pairs = [jnp.concatenate([parts[2 * i], parts[2 * i + 1]], axis=1) for i in range(X // 2)]
    for x in range(X):
        total = base[x]
        for i, pair in enumerate(pairs):
            total = total + jnp.dot(pair, weight[x, i], preferred_element_type=jnp.float32)
        out[x] = jnp.maximum(total, 0.0).astype(out.dtype) if last else total


def add_product(base, parts, weight, last=False):
    vmem = pl.BlockSpec(memory_space=pltpu.VMEM)
    return pl.pallas_call(
        functools.partial(product_kernel, last),
        out_shape=jax.ShapeDtypeStruct(base.shape, jnp.bfloat16 if last else jnp.float32),
        in_specs=[vmem] * 3,
        out_specs=vmem,
        compiler_params=pltpu.CompilerParams(vmem_limit_bytes=16 * 1024 * 1024),
        cost_estimate=pl.CostEstimate(flops=base.size * 1024, bytes_accessed=2 * 2**20, transcendentals=0),
        name="add_product",
    )(parts, weight, base)


def rows_of_core(weights, core):
    parts = weights.reshape(X, X, CORE, BLK, BLK)
    return jnp.where(core == 0, parts[:, :, 0], parts[:, :, 1]).reshape(X, X // 2, 2 * BLK, BLK)


def to_all(array, axis, size):
    return lax.all_to_all(jnp.broadcast_to(array[None], (size,) + array.shape), axis, 0, 0, tiled=True)


def swap_cores(array):
    return lax.ppermute(array, "core", [(0, 1), (1, 0)])


def of_ring(array, x):
    came = [array] + [lax.ppermute(array, "x", [(i, (i + r) % X) for i in range(X)]) for r in range(1, X)]
    return jnp.stack(came)[(x - jnp.arange(X)) % X]


def body(
    features,
    history,
    w_root,
    w_neigh,
    bias,
    local_tiles,
    halo_tiles,
    local_src,
    halo_src,
    halo_count,
    halo_peer,
    halo_block,
):
    rows, columns = features.shape
    my_z, my_y, my_core = lax.axis_index("z"), lax.axis_index("y"), lax.axis_index("core")

    column_blocks = lax.all_gather(history, "z", axis=0, tiled=True)

    depth = w_root.shape[0]
    bias_rows = jnp.pad(bias[None], ((0, META - 1), (0, 0)))
    weights = of_ring(jnp.concatenate([w_root, w_neigh, bias_rows]), lax.axis_index("x"))
    root, neigh, bias_row = weights[:, :depth], weights[:, depth : 2 * depth], weights[:, 2 * depth : 2 * depth + 1]

    owners = (my_z * Y + my_y + 1 + halo_peer[:, 0]) % (Z * Y)
    hits = halo_src.reshape(REFS, 1) == jnp.arange(halo_block.shape[0], dtype=jnp.int32)[None, :]
    used = (lax.broadcasted_iota(jnp.int32, (TB, HT), 1) < halo_count[:, None]).reshape(REFS)
    code = jnp.sum(jnp.where(hits, (owners * TB + halo_block)[None, :], 0), axis=1)
    code = jnp.where(used, code, -TB)
    notes = jnp.stack([code // TB, code % TB])
    notes = jnp.pad(notes, ((0, META - 2), (0, BLK - REFS))).astype(jnp.bfloat16)
    share = lax.dynamic_slice_in_dim(halo_tiles.reshape(REFS * BLK, BLK), my_core * HALF * BLK, HALF * BLK)
    mine = to_all(jnp.concatenate([share, notes]), "y", Y)
    other = swap_cores(mine)
    told = mine[:, HALF * BLK : HALF * BLK + 2, :REFS].astype(jnp.int32).reshape(Y, 2 * REFS)
    place = jnp.stack([my_y, my_core])

    own_blocks = features.reshape(TB, BLK, columns)[local_src]
    local_part = jnp.einsum("bij,bjc->bic", local_tiles, own_blocks, preferred_element_type=jnp.float32)
    quarter = (X, rows // X, columns)
    mine_f = lax.all_to_all(features.reshape(quarter), "x", 0, 0, tiled=True)
    other_f = swap_cores(mine_f)
    base = jnp.broadcast_to(bias_row.astype(jnp.float32), quarter)
    base = add_product(base, mine_f, rows_of_core(root, my_core))
    base = add_product(base, other_f, rows_of_core(root, 1 - my_core))
    neigh_mine, neigh_other = rows_of_core(neigh, my_core), rows_of_core(neigh, 1 - my_core)
    column_blocks, base, local_part, neigh_mine, neigh_other = lax.optimization_barrier(
        (column_blocks, base, local_part, neigh_mine, neigh_other)
    )

    sent = partial_sums(told, place, column_blocks, local_part, mine, other)
    came = lax.all_to_all(sent.reshape((Y * X,) + quarter[1:]), ("y", "x"), 0, 0, tiled=True).astype(jnp.float32)
    aggregate = sum(came[y * X : (y + 1) * X] for y in range(Y)).astype(jnp.bfloat16)
    other_a = swap_cores(aggregate)
    base = add_product(base, aggregate, neigh_mine)
    out = add_product(base, other_a, neigh_other, last=True)
    return lax.all_to_all(out, "x", 0, 0, tiled=True).reshape(rows, columns)


def solution(mesh):
    chips = Mesh(mesh.devices.reshape(Z, Y, X, CORE), ("z", "y", "x", "core"))
    dom, feat = ("z", "y"), ("x", "core")
    in_specs = (
        P(dom, feat),
        P(dom, feat),
        P(None, feat),
        P(None, feat),
        P(feat),
        P(dom, None, None),
        P(dom, None, None, None),
        P(dom),
        P(dom, None),
        P(dom),
        P(dom, None),
        P(dom),
    )
    return jax.shard_map(body, mesh=chips, in_specs=in_specs, out_specs=P(dom, feat), check_vma=False)
```

```python
import functools

import jax
import jax.numpy as jnp
from jax import lax
from jax.experimental import pallas as pl
from jax.experimental.pallas import tpu as pltpu
from jax.sharding import Mesh
from jax.sharding import PartitionSpec as P

Z, Y, X, CORE = 16, 4, 4, 2
BLK = 128
TB = 8
HT = 3
REFS = TB * HT
HALF = REFS // CORE
META = 16
GROUP = 4


def pick_kernel(notes, place, mine, other, table, picked, buf, sem, out_sem):
    me, core = place[0], place[1]
    counts = []
    for peer in range(Y):

        def step(ref, count):
            owner, block = notes[peer, ref], notes[peer, REFS + ref]
            here = jnp.logical_and(owner >= 0, lax.rem(owner, Y) == me)
            at = pl.ds(pl.multiple_of(lax.rem(ref, HALF) * BLK, BLK), BLK)
            from_mine = lax.div(ref, HALF) == core

            @pl.when(here)
            def _():
                table[peer, count] = lax.div(owner, Y) * TB + block
                table[peer, REFS + count] = peer * TB + lax.div(ref, HT)

            @pl.when(jnp.logical_and(here, from_mine))
            def _():
                pltpu.make_async_copy(mine.at[peer, at], buf.at[peer, count], sem.at[peer, count]).start()

            @pl.when(jnp.logical_and(here, jnp.logical_not(from_mine)))
            def _():
                pltpu.make_async_copy(other.at[peer, at], buf.at[peer, count], sem.at[peer, count]).start()

            return count + here.astype(jnp.int32)

        count = lax.fori_loop(0, REFS, step, jnp.int32(0))
        counts.append(count)
        table[peer, 2 * REFS] = count
        table[peer, 2 * REFS + 1] = me

        @pl.loop(count, REFS)
        def _(i):
            table[peer, i] = 0
            table[peer, REFS + i] = Y * TB

    def out_copy(peer, group):
        at = pl.ds(group * GROUP, GROUP)
        return pltpu.make_async_copy(buf.at[peer, at], picked.at[peer, at], out_sem.at[peer, group])

    for peer in range(Y):

        @pl.loop(0, (counts[peer] + GROUP - 1) // GROUP)
        def _(group):
            for u in range(GROUP):
                i = group * GROUP + u

                @pl.when(i < counts[peer])
                def _():
                    pltpu.make_async_copy(mine.at[peer, pl.ds(0, BLK)], buf.at[peer, i], sem.at[peer, i]).wait()

            out_copy(peer, group).start()

    for peer in range(Y):

        @pl.loop(0, (counts[peer] + GROUP - 1) // GROUP)
        def _(group):
            out_copy(peer, group).wait()


def partial_kernel(
    table, blocks, tiles, local, sent, block_buf, tile_buf, local_buf, total, block_sem, tile_sem, local_sem
):
    count = [table[peer, 2 * REFS] for peer in range(Y)]
    me = table[0, 2 * REFS + 1]

    def groups(peer):
        return (count[peer] + GROUP - 1) // GROUP

    def block_copy(peer, i):
        row = pl.multiple_of(table[peer, i] * BLK, BLK)
        return pltpu.make_async_copy(blocks.at[pl.ds(row, BLK)], block_buf.at[peer, i], block_sem.at[peer, i])

    def tile_copy(peer, group):
        at = pl.ds(group * GROUP, GROUP)
        return pltpu.make_async_copy(tiles.at[peer, at], tile_buf.at[peer, at], tile_sem.at[peer, group])

    for peer in range(Y):

        @pl.loop(0, groups(peer))
        def _(group):
            for u in range(GROUP):
                i = group * GROUP + u

                @pl.when(i < count[peer])
                def _():
                    block_copy(peer, i).start()

            tile_copy(peer, group).start()

    local_copy = pltpu.make_async_copy(local, local_buf, local_sem)
    local_copy.start()
    total[pl.ds(0, Y * TB)] = jnp.zeros((Y * TB, BLK, BLK), jnp.float32)
    for peer in range(Y):

        @pl.loop(0, groups(peer))
        def _(group):
            members = [group * GROUP + u for u in range(GROUP)]
            tile_copy(peer, group).wait()
            for i in members:

                @pl.when(i < count[peer])
                def _():
                    block_copy(peer, i).wait()

            products = [
                jnp.dot(tile_buf[peer, i], block_buf[peer, i], preferred_element_type=jnp.float32) for i in members
            ]
            for i, part in zip(members, products):
                total[table[peer, REFS + i]] += part

        @pl.when(me == peer)
        def _():
            local_copy.wait()
            total[pl.ds(peer * TB, TB)] += local_buf[...]

        at = pl.ds(peer * TB, TB)
        sent[at] = total[at].astype(sent.dtype)


def partial_sums(notes, place, blocks, local, mine, other):
    smem, hbm = pl.BlockSpec(memory_space=pltpu.SMEM), pl.BlockSpec(memory_space=pltpu.HBM)
    table, picked = pl.pallas_call(
        pick_kernel,
        out_shape=(
            jax.ShapeDtypeStruct((Y, 2 * REFS + 2), jnp.int32),
            jax.ShapeDtypeStruct((Y, REFS, BLK, BLK), jnp.bfloat16),
        ),
        in_specs=[smem] * 2 + [hbm] * 2,
        out_specs=(smem, hbm),
        scratch_shapes=[
            pltpu.VMEM((Y, REFS, BLK, BLK), jnp.bfloat16),
            pltpu.SemaphoreType.DMA((Y, REFS)),
            pltpu.SemaphoreType.DMA((Y, REFS // GROUP)),
        ],
        compiler_params=pltpu.CompilerParams(vmem_limit_bytes=8 * 1024 * 1024),
        cost_estimate=pl.CostEstimate(flops=0, bytes_accessed=4 * 2**20, transcendentals=0),
        name="pick_tiles",
    )(notes, place, mine, other)
    return pl.pallas_call(
        partial_kernel,
        out_shape=jax.ShapeDtypeStruct((Y * TB, BLK, BLK), jnp.bfloat16),
        in_specs=[smem] + [hbm] * 3,
        out_specs=pl.BlockSpec(memory_space=pltpu.VMEM),
        scratch_shapes=[
            pltpu.VMEM((Y, REFS, BLK, BLK), jnp.bfloat16),
            pltpu.VMEM((Y, REFS, BLK, BLK), jnp.bfloat16),
            pltpu.VMEM((TB, BLK, BLK), jnp.float32),
            pltpu.VMEM((Y * TB + 1, BLK, BLK), jnp.float32),
            pltpu.SemaphoreType.DMA((Y, REFS)),
            pltpu.SemaphoreType.DMA((Y, REFS // GROUP)),
            pltpu.SemaphoreType.DMA,
        ],
        compiler_params=pltpu.CompilerParams(vmem_limit_bytes=60 * 1024 * 1024),
        cost_estimate=pl.CostEstimate(flops=REFS * 2 * BLK**3, bytes_accessed=4 * 2**20, transcendentals=0),
        name="partial_sums",
    )(table, blocks, picked, local)


def product_kernel(last, parts, weight, base, out):
    pairs = [jnp.concatenate([parts[2 * i], parts[2 * i + 1]], axis=1) for i in range(X // 2)]
    for x in range(X):
        total = base[x]
        for i, pair in enumerate(pairs):
            total = total + jnp.dot(pair, weight[x, i], preferred_element_type=jnp.float32)
        out[x] = jnp.maximum(total, 0.0).astype(out.dtype) if last else total


def add_product(base, parts, weight, last=False):
    vmem = pl.BlockSpec(memory_space=pltpu.VMEM)
    return pl.pallas_call(
        functools.partial(product_kernel, last),
        out_shape=jax.ShapeDtypeStruct(base.shape, jnp.bfloat16 if last else jnp.float32),
        in_specs=[vmem] * 3,
        out_specs=vmem,
        compiler_params=pltpu.CompilerParams(vmem_limit_bytes=16 * 1024 * 1024),
        cost_estimate=pl.CostEstimate(flops=base.size * 1024, bytes_accessed=2 * 2**20, transcendentals=0),
        name="add_product",
    )(parts, weight, base)


def rows_of_core(weights, core):
    parts = weights.reshape(X, X, CORE, BLK, BLK)
    return jnp.where(core == 0, parts[:, :, 0], parts[:, :, 1]).reshape(X, X // 2, 2 * BLK, BLK)


def to_all(array, axis, size):
    return lax.all_to_all(jnp.broadcast_to(array[None], (size,) + array.shape), axis, 0, 0, tiled=True)


def swap_cores(array):
    return lax.ppermute(array, "core", [(0, 1), (1, 0)])


def of_ring(array, x):
    came = [array] + [lax.ppermute(array, "x", [(i, (i + r) % X) for i in range(X)]) for r in range(1, X)]
    return jnp.stack(came)[(x - jnp.arange(X)) % X]


def body(
    features,
    history,
    w_root,
    w_neigh,
    bias,
    local_tiles,
    halo_tiles,
    local_src,
    halo_src,
    halo_count,
    halo_peer,
    halo_block,
):
    rows, columns = features.shape
    my_z, my_y, my_core = lax.axis_index("z"), lax.axis_index("y"), lax.axis_index("core")

    column_blocks = lax.all_gather(history, "z", axis=0, tiled=True)

    depth = w_root.shape[0]
    bias_rows = jnp.pad(bias[None], ((0, META - 1), (0, 0)))
    weights = of_ring(jnp.concatenate([w_root, w_neigh, bias_rows]), lax.axis_index("x"))
    root, neigh, bias_row = weights[:, :depth], weights[:, depth : 2 * depth], weights[:, 2 * depth : 2 * depth + 1]

    owners = (my_z * Y + my_y + 1 + halo_peer[:, 0]) % (Z * Y)
    hits = halo_src.reshape(REFS, 1) == jnp.arange(halo_block.shape[0], dtype=jnp.int32)[None, :]
    used = (lax.broadcasted_iota(jnp.int32, (TB, HT), 1) < halo_count[:, None]).reshape(REFS)
    code = jnp.sum(jnp.where(hits, (owners * TB + halo_block)[None, :], 0), axis=1)
    code = jnp.where(used, code, -TB)
    notes = jnp.stack([code // TB, code % TB])
    notes = jnp.pad(notes, ((0, META - 2), (0, BLK - REFS))).astype(jnp.bfloat16)
    share = lax.dynamic_slice_in_dim(halo_tiles.reshape(REFS * BLK, BLK), my_core * HALF * BLK, HALF * BLK)
    mine = to_all(jnp.concatenate([share, notes]), "y", Y)
    other = swap_cores(mine)
    told = mine[:, HALF * BLK : HALF * BLK + 2, :REFS].astype(jnp.int32).reshape(Y, 2 * REFS)
    place = jnp.stack([my_y, my_core])

    own_blocks = features.reshape(TB, BLK, columns)[local_src]
    local_part = jnp.einsum("bij,bjc->bic", local_tiles, own_blocks, preferred_element_type=jnp.float32)
    quarter = (X, rows // X, columns)
    mine_f = lax.all_to_all(features.reshape(quarter), "x", 0, 0, tiled=True)
    other_f = swap_cores(mine_f)
    base = jnp.broadcast_to(bias_row.astype(jnp.float32), quarter)
    base = add_product(base, mine_f, rows_of_core(root, my_core))
    base = add_product(base, other_f, rows_of_core(root, 1 - my_core))
    neigh_mine, neigh_other = rows_of_core(neigh, my_core), rows_of_core(neigh, 1 - my_core)
    column_blocks, base, local_part, neigh_mine, neigh_other = lax.optimization_barrier(
        (column_blocks, base, local_part, neigh_mine, neigh_other)
    )

    sent = partial_sums(told, place, column_blocks, local_part, mine, other)
    came = lax.all_to_all(sent.reshape((Y * X,) + quarter[1:]), ("y", "x"), 0, 0, tiled=True).astype(jnp.float32)
    aggregate = sum(came[y * X : (y + 1) * X] for y in range(Y)).astype(jnp.bfloat16)
    other_a = swap_cores(aggregate)
    base = add_product(base, aggregate, neigh_mine)
    out = add_product(base, other_a, neigh_other, last=True)
    return lax.all_to_all(out, "x", 0, 0, tiled=True).reshape(rows, columns)


def solution(mesh):
    chips = Mesh(mesh.devices.reshape(Z, Y, X, CORE), ("z", "y", "x", "core"))
    dom, feat = ("z", "y"), ("x", "core")
    in_specs = (
        P(dom, feat),
        P(dom, feat),
        P(None, feat),
        P(None, feat),
        P(feat),
        P(dom, None, None),
        P(dom, None, None, None),
        P(dom),
        P(dom, None),
        P(dom),
        P(dom, None),
        P(dom),
    )
    return jax.shard_map(body, mesh=chips, in_specs=in_specs, out_specs=P(dom, feat), check_vma=False)
```
